256 devices in a mesh: grp: 8 (over x, core), seq: 32 (over z, y).
Axes of the slice: x: 4, y: 4, z: 8, core: 2. Of those that a mesh axis runs over, the one named last changes fastest.
Arguments:
- queries: bfloat16 [32, 2048, 4096], P('grp', 'seq'), may hold values from -24 to 24
- key_tokens: bfloat16 [32, 2048, 4096], P('grp', 'seq'), may hold values from -24 to 24
- value_tokens: bfloat16 [32, 2048, 4096], P('grp', 'seq'), may hold values from -6 to 6
- clip_lengths: int32 [32], replicated, may hold values from 1 to 2048, as said below
Outputs:
- attended: bfloat16 [32, 2048, 4096], P('grp', 'seq')
The draws below stay inside these ranges and needn't reach their ends.
Inputs may be any that keep to these rules, and one draw needn't show every extreme that they name: `clip_lengths`: some clip has exactly 2048 valid tokens and some clip exactly 1.
All inputs are finite; a program needn't handle non-finite values.
Results may differ from the reference program's by a relative error of at most 0.0036.
Values may be sent and summed in bfloat16 or wider, within the bound.
No kernel may reach another device: no remote copies, remote signals or barrier semaphores. Data moves between devices by JAX's collectives and lax.ppermute only.
A program may use at most 64 MiB of HBM per device.

```python
import jax
import jax.numpy as jnp
from jax import lax

H = 32
HD = 128
LMAX = 2048
CG = 4
CLIPS = 32


def draw_queries(key, part):
    key = jax.random.fold_in(key, 1)
    result = 2.0 * jnp.clip(jax.random.normal(key, (CLIPS, LMAX, H * HD), jnp.float32), -5.0, 5.0)
    return result.astype(jnp.bfloat16)


def draw_key_tokens(key, part):
    key = jax.random.fold_in(key, 2)
    result = jnp.clip(jax.random.normal(key, (CLIPS, LMAX, H * HD), jnp.float32), -5.0, 5.0)
    return result.astype(jnp.bfloat16)


def draw_clip_lengths(key, part):
    key = jax.random.fold_in(key, 3)
    length_key, group_key, pick_key = jax.random.split(key, 3)
    drawn_lengths = jax.random.randint(length_key, (CLIPS,), 1, LMAX + 1, jnp.int32)
    light_group = jax.random.randint(group_key, (CLIPS // CG,), 0, 2, jnp.int32)
    light_clip = jnp.repeat(light_group, CG)
    lengths_out = jnp.where(light_clip == 1, drawn_lengths // 4 + 1, drawn_lengths)
    chosen = jax.random.permutation(pick_key, CLIPS)
    lengths_out = lengths_out.at[chosen[0]].set(LMAX).at[chosen[1]].set(1)
    return lengths_out.astype(jnp.int32)


def steps_of(own_key, extent, cuts, low, top_value):
    level = 1.0
    for position, blocks in cuts:
        heights = jax.random.uniform(jax.random.fold_in(jax.random.fold_in(own_key, 6), position), (blocks,), jnp.float32, low / len(cuts), top_value / len(cuts))
        level = level * jnp.repeat(jnp.exp(heights), extent[position] // blocks).reshape((-1,) + (1,) * (len(extent) - 1 - position))
    return level


def normal_values(rng, shape, deviation, reach, cuts=(), held_as=jnp.bfloat16):
    values = jax.random.normal(rng, shape, jnp.float32) * deviation
    if len(cuts) > 0:
        values = steps_of(rng, shape, cuts, -0.22, 0.18) * values
    return jnp.clip(values, min=-reach, max=reach).astype(held_as)


def setup_inputs(seed: int = 0) -> dict:
    arg_keys = jax.random.split(jax.random.key(seed), 5)
    queries = draw_queries(jax.random.fold_in(arg_keys[4], 71), 0)
    key_tokens = draw_key_tokens(jax.random.fold_in(arg_keys[4], 71), 0)
    value_tokens = normal_values(arg_keys[2], (CLIPS, LMAX, H * HD), 1.0, 6.0, ((0, 8), (1, 32)))
    clip_lengths = draw_clip_lengths(jax.random.fold_in(arg_keys[4], 71), 0)
    return {"queries": queries, "key_tokens": key_tokens, "value_tokens": value_tokens, "clip_lengths": clip_lengths}


def clip_attention(inputs):
    query_rows, key_rows, value_rows, clip_length = inputs
    shaped_q = query_rows.astype(jnp.float32).reshape(LMAX, H, HD)
    shaped_k = key_rows.astype(jnp.float32).reshape(LMAX, H, HD)
    shaped_v = value_rows.astype(jnp.float32).reshape(LMAX, H, HD)
    scores = jnp.einsum("qhd,khd->hqk", shaped_q, shaped_k) * (HD ** -0.5)
    positions = jnp.arange(LMAX, dtype=jnp.int32)
    key_valid = positions < clip_length
    scores = jnp.where(key_valid[None, None, :], scores, -jnp.inf)
    row_max = jnp.max(scores, axis=-1, keepdims=True)
    exp_scores = jnp.where(key_valid[None, None, :], jnp.exp(scores - row_max), 0.0)
    row_total = jnp.sum(exp_scores, axis=-1)
    weights = lax.optimization_barrier(exp_scores.astype(jnp.bfloat16))
    weighted = jnp.einsum("hqk,khd->qhd", weights.astype(jnp.float32), shaped_v)
    weighted = weighted / jnp.transpose(row_total)[:, :, None]
    weighted = jnp.where(key_valid[:, None, None], weighted, 0.0)
    return weighted.reshape(LMAX, H * HD).astype(jnp.bfloat16)


def reference(queries, key_tokens, value_tokens, clip_lengths):
    return lax.map(clip_attention, (queries, key_tokens, value_tokens, clip_lengths))
```

```python
import jax
import jax.numpy as jnp
from jax import lax
from jax.experimental import pallas as pl
from jax.experimental.pallas import tpu as pltpu
from jax.sharding import PartitionSpec as P

HD = 128
EXP2_SCALE = HD ** (-0.5) * 1.4426950408889634
BLOCK = 512
PIECE = 64
WIDE, NEAR, NEAREST = 32, 8, 4
VMEM_LIMIT = 24 * 2**20


def in_hbm(array):
    return pltpu.with_memory_space_constraint(array, pltpu.HBM)


def by_length(lengths_ref, group_ref, per_group, rank):
    lengths = [lengths_ref[group_ref[0] * per_group + slot] for slot in range(per_group)]
    slot_at_rank, length_at_rank = jnp.int32(0), jnp.int32(0)
    for slot in range(per_group):
        place = jnp.int32(0)
        for other in range(per_group):
            if other < slot:
                place += (lengths[other] >= lengths[slot]).astype(jnp.int32)
            elif other > slot:
                place += (lengths[other] > lengths[slot]).astype(jnp.int32)
        slot_at_rank = jnp.where(place == rank, slot, slot_at_rank)
        length_at_rank = jnp.where(place == rank, lengths[slot], length_at_rank)
    return slot_at_rank, length_at_rank


def pack(lengths, group, first, clips, queries, keys, values):
    per_group, rows, features = queries.shape
    heads = features // HD

    def kernel(lengths_ref, group_ref, q_ref, k_ref, v_ref, out_ref, held, sems):
        def fetch(clip, position):
            slot = by_length(lengths_ref, group_ref, per_group, first + clip)[0]
            source = (q_ref, k_ref, v_ref)[position].at[slot]
            return pltpu.make_async_copy(source, held.at[clip, position], sems.at[clip, position])

        clip = pl.program_id(0)

        @pl.when(clip == 0)
        def _():
            for each in range(clips):
                for position in range(3):
                    fetch(each, position).start()

        for position in range(3):
            fetch(clip, position).wait()

        def by_head(head, carry):
            columns = pl.ds(pl.multiple_of(head * HD, HD), HD)
            for position in range(3):
                out_ref[head, position, 0] = held[clip, position, :, columns]
            return carry

        lax.fori_loop(0, heads, by_head, 0, unroll=4)

    return pl.pallas_call(
        kernel,
        grid_spec=pltpu.PrefetchScalarGridSpec(
            num_scalar_prefetch=2,
            grid=(clips,),
            in_specs=[pl.BlockSpec(memory_space=pltpu.HBM)] * 3,
            out_specs=pl.BlockSpec((heads, 3, 1, rows, HD), lambda c, ln, gr: (0, 0, c, 0, 0)),
            scratch_shapes=[
                pltpu.VMEM((clips, 3, rows, features), queries.dtype),
                pltpu.SemaphoreType.DMA((clips, 3)),
            ],
        ),
        out_shape=pltpu.HBM((heads, 3, clips, rows, HD), queries.dtype),
        compiler_params=pltpu.CompilerParams(vmem_limit_bytes=VMEM_LIMIT),
        name="pack",
    )(in_hbm(lengths), group, in_hbm(queries), in_hbm(keys), in_hbm(values))


def attend_head(head, count, q_ref, k_ref, v_ref, out_ref, scratch):
    values_ref, score_ref, max_ref, low_ref, high_ref, summed_ref = scratch
    rows_each = q_ref.shape[4]
    block_rows = score_ref.shape[1]
    half_rows = block_rows // 2
    pieces = block_rows // rows_each
    blocks = (count + block_rows - 1) // block_rows
    halves = [slice(0, half_rows), slice(half_rows, block_rows)]

    def score_block(query_rows, block, masked):
        key_rows = k_ref[pl.ds(block * pieces, pieces), head].reshape(block_rows, HD)
        for half in halves:
            scores = lax.dot_general(
                query_rows[half], key_rows, (((1,), (1,)), ((), ())), preferred_element_type=jnp.float32
            )
            if masked:
                columns = block * block_rows + lax.broadcasted_iota(jnp.int32, (1, block_rows), 1)
                scores = jnp.where(columns < count, scores, -jnp.inf)
            score_ref[block, half, :] = scores
            lane_max = scores[:, :HD]
            for start in range(HD, block_rows, HD):
                lane_max = jnp.maximum(lane_max, scores[:, start : start + HD])
            max_ref[half, :] = jnp.maximum(max_ref[half, :], lane_max)

    def weight_block(block, carry):
        value_rows = values_ref[pl.ds(pl.multiple_of(block * block_rows, block_rows), block_rows)]
        for half, weight_ref in zip(halves, (low_ref, high_ref)):
            for row in range(0, half_rows, PIECE):
                rows = slice(half.start + row, half.start + row + PIECE)
                row_max = max_ref[rows, :]
                for start in range(0, block_rows, HD):
                    scores = score_ref[block, rows, start : start + HD]
                    weights = jnp.exp2((scores - row_max) * EXP2_SCALE)
                    weight_ref[row : row + PIECE, start : start + HD] = weights.astype(weight_ref.dtype)
            summed_ref[half, :] += jnp.dot(weight_ref[...], value_rows, preferred_element_type=jnp.float32)
        return carry

    def tile(step, carry):
        at = pl.ds(step * pieces, pieces)
        query_rows = q_ref[at, head].reshape(block_rows, HD)
        max_ref[...] = jnp.full_like(max_ref, -jnp.inf)

        def whole_block(block, inner):
            score_block(query_rows, block, False)
            return inner

        lax.fori_loop(0, blocks - 1, whole_block, 0)
        score_block(query_rows, blocks - 1, True)
        max_ref[...] = jnp.broadcast_to(jnp.max(max_ref[...], axis=1, keepdims=True), max_ref.shape)
        summed_ref[...] = jnp.zeros_like(summed_ref)
        lax.fori_loop(0, blocks, weight_block, 0)
        rows = step * block_rows + lax.broadcasted_iota(jnp.int32, (block_rows, HD), 0)
        attended = jnp.where(rows < count, summed_ref[:, :HD] / summed_ref[:, HD:], 0.0)
        out_ref[at, head] = attended.astype(out_ref.dtype).reshape(pieces, 1, rows_each, HD)
        return carry

    values_ref[:, :HD] = v_ref[:, head].reshape(values_ref.shape[0], HD)
    lax.fori_loop(0, blocks, tile, 0)


def attend(lengths, group, place, first, clips, sources, per_group, arrived):
    heads, rows = arrived.shape[0] // sources, arrived.shape[3]
    held_rows = sources * rows
    block_rows = min(BLOCK, held_rows)
    arrived = arrived.reshape(sources, heads, 3, clips, rows, HD)
    whole = lambda position: pl.BlockSpec(
        (sources, heads, 1, 1, rows, HD), lambda c, ln, gr, at: (0, 0, position, c, 0, 0)
    )

    def kernel(lengths_ref, group_ref, place_ref, q_ref, k_ref, v_ref, out_ref, *scratch):
        count = by_length(lengths_ref, group_ref, per_group, first + pl.program_id(0))[1]
        count = jnp.where(place_ref[0] < sources, count, 0)
        out_ref[...] = jnp.zeros_like(out_ref)

        @pl.when(pl.program_id(0) == 0)
        def _():
            scratch[0][:, HD:] = jnp.ones((held_rows, HD), scratch[0].dtype)

        def by_head(head, carry):
            attend_head(head, count, q_ref, k_ref, v_ref, out_ref, scratch)
            return carry

        @pl.when(count > 0)
        def _():
            lax.fori_loop(0, heads, by_head, 0)

    attended = pl.pallas_call(
        kernel,
        grid_spec=pltpu.PrefetchScalarGridSpec(
            num_scalar_prefetch=3,
            grid=(clips,),
            in_specs=[whole(0), whole(1), whole(2)],
            out_specs=pl.BlockSpec(
                (sources, heads, 1, rows, HD), lambda c, ln, gr, at: (0, 0, c, 0, 0)
            ),
            scratch_shapes=[
                pltpu.VMEM((held_rows, 2 * HD), arrived.dtype),
                pltpu.VMEM((held_rows // block_rows, block_rows, block_rows), jnp.float32),
                pltpu.VMEM((block_rows, HD), jnp.float32),
                pltpu.VMEM((block_rows // 2, block_rows), arrived.dtype),
                pltpu.VMEM((block_rows // 2, block_rows), arrived.dtype),
                pltpu.VMEM((block_rows, 2 * HD), jnp.float32),
            ],
        ),
        out_shape=pltpu.HBM((sources, heads, clips, rows, HD), arrived.dtype),
        compiler_params=pltpu.CompilerParams(vmem_limit_bytes=VMEM_LIMIT),
        name="attend",
    )(in_hbm(lengths), group, place, arrived, arrived, arrived)
    return attended.reshape(sources * heads, clips, rows, HD)


def unpack(lengths, group, parts, returned):
    heads, _, rows, _ = returned[0].shape
    per_group = sum(clips for _, clips, _ in parts)

    def kernel(lengths_ref, group_ref, *refs):
        out_ref = refs[-1]
        rank = pl.program_id(0)
        for (first, clips, _), in_ref in zip(parts, refs):

            @pl.when((rank >= first) & (rank < first + clips))
            def _(in_ref=in_ref):

                def by_head(head, carry):
                    out_ref[0, :, pl.ds(pl.multiple_of(head * HD, HD), HD)] = in_ref[head, 0]
                    return carry

                lax.fori_loop(0, heads, by_head, 0, unroll=4)

    return pl.pallas_call(
        kernel,
        grid_spec=pltpu.PrefetchScalarGridSpec(
            num_scalar_prefetch=2,
            grid=(per_group,),
            in_specs=[
                pl.BlockSpec(
                    (heads, 1, rows, HD),
                    lambda c, ln, gr, first=first, clips=clips: (0, jnp.clip(c - first, 0, clips - 1), 0, 0),
                )
                for first, clips, _ in parts
            ],
            out_specs=pl.BlockSpec(
                (1, rows, heads * HD), lambda c, ln, gr: (by_length(ln, gr, per_group, c)[0], 0, 0)
            ),
        ),
        out_shape=pltpu.HBM((per_group, rows, heads * HD), returned[0].dtype),
        compiler_params=pltpu.CompilerParams(vmem_limit_bytes=VMEM_LIMIT),
        name="unpack",
    )(in_hbm(lengths), group, *returned)


def exchange(array, peers):
    devices = lax.axis_size("seq")
    blocks = [list(range(start, start + peers)) for start in range(0, devices, peers)]
    return lax.all_to_all(
        array, "seq", split_axis=0, concat_axis=0, axis_index_groups=blocks, tiled=True
    )


def planned(parts):
    def run(queries, keys, values, lengths, group, place):
        per_group = queries.shape[0]
        arrived, before = [], None
        for first, clips, peers in parts:
            packed = pack(lengths, group, first, clips, queries, keys, values)
            if before is not None:
                packed, before = lax.optimization_barrier((packed, before))
                arrived[-1] = before
            before = exchange(packed, peers)
            arrived.append(before)
        returned = []
        for (first, clips, peers), rows in zip(parts, arrived):
            attended = attend(lengths, group, place, first, clips, peers, per_group, rows)
            attended, before = lax.optimization_barrier((attended, before))
            before = exchange(attended, peers)
            returned.append(before)
        return unpack(lengths, group, parts, returned)

    return run


PLANS = (
    ((0, 4, NEAR),),
    ((0, 2, NEAR), (2, 2, NEAREST)),
    ((2, 2, NEAR), (0, 2, WIDE)),
    ((0, 2, WIDE), (2, 2, NEAR)),
    ((3, 1, NEAR), (0, 3, WIDE)),
    ((0, 3, WIDE), (3, 1, NEAR)),
    ((0, 2, WIDE), (2, 2, WIDE)),
    ((0, 3, WIDE), (3, 1, WIDE)),
)


def local(queries, key_tokens, value_tokens, clip_lengths):
    per_group, rows = queries.shape[:2]
    group, place = lax.axis_index("grp"), lax.axis_index("seq")
    counts = lax.dynamic_slice(clip_lengths, (group * per_group,), (per_group,))
    long = jnp.sum((counts > NEAR * rows).astype(jnp.int32))
    tiny = jnp.sum((counts <= NEAREST * rows).astype(jnp.int32))
    with_long = 2 * jnp.maximum(long - 1, 1) + group % 2
    chosen = jnp.where(long > 0, with_long, jnp.where(tiny >= 2, 1, 0))
    return lax.switch(
        chosen,
        [planned(parts) for parts in PLANS],
        queries, key_tokens, value_tokens, clip_lengths, group.reshape(1), place.reshape(1),
    )


def solution(mesh):
    in_specs = (P("grp", "seq", None), P("grp", "seq", None), P("grp", "seq", None), P())
    out_specs = P("grp", "seq", None)
    return jax.shard_map(local, mesh=mesh, in_specs=in_specs, out_specs=out_specs, check_vma=False)
```

```python
import jax
import jax.numpy as jnp
from jax import lax
from jax.experimental import pallas as pl
from jax.experimental.pallas import tpu as pltpu
from jax.sharding import PartitionSpec as P

HD = 128
EXP2_SCALE = HD ** (-0.5) * 1.4426950408889634
BLOCK = 512
PIECE = 64
WIDE, NEAR, NEAREST = 32, 8, 4
VMEM_LIMIT = 24 * 2**20


def in_hbm(array):
    return pltpu.with_memory_space_constraint(array, pltpu.HBM)


def by_length(lengths_ref, group_ref, per_group, rank):
    lengths = [lengths_ref[group_ref[0] * per_group + slot] for slot in range(per_group)]
    slot_at_rank, length_at_rank = jnp.int32(0), jnp.int32(0)
    for slot in range(per_group):
        place = jnp.int32(0)
        for other in range(per_group):
            if other < slot:
                place += (lengths[other] >= lengths[slot]).astype(jnp.int32)
            elif other > slot:
                place += (lengths[other] > lengths[slot]).astype(jnp.int32)
        slot_at_rank = jnp.where(place == rank, slot, slot_at_rank)
        length_at_rank = jnp.where(place == rank, lengths[slot], length_at_rank)
    return slot_at_rank, length_at_rank


def pack(lengths, group, first, clips, queries, keys, values):
    per_group, rows, features = queries.shape
    heads = features // HD

    def kernel(lengths_ref, group_ref, q_ref, k_ref, v_ref, out_ref, held, sems):
        def fetch(clip, position):
            slot = by_length(lengths_ref, group_ref, per_group, first + clip)[0]
            source = (q_ref, k_ref, v_ref)[position].at[slot]
            return pltpu.make_async_copy(source, held.at[clip, position], sems.at[clip, position])

        clip = pl.program_id(0)

        @pl.when(clip == 0)
        def _():
            for each in range(clips):
                for position in range(3):
                    fetch(each, position).start()

        for position in range(3):
            fetch(clip, position).wait()

        def by_head(head, carry):
            columns = pl.ds(pl.multiple_of(head * HD, HD), HD)
            for position in range(3):
                out_ref[head, position, 0] = held[clip, position, :, columns]
            return carry

        lax.fori_loop(0, heads, by_head, 0, unroll=4)

    return pl.pallas_call(
        kernel,
        grid_spec=pltpu.PrefetchScalarGridSpec(
            num_scalar_prefetch=2,
            grid=(clips,),
            in_specs=[pl.BlockSpec(memory_space=pltpu.HBM)] * 3,
            out_specs=pl.BlockSpec((heads, 3, 1, rows, HD), lambda c, ln, gr: (0, 0, c, 0, 0)),
            scratch_shapes=[
                pltpu.VMEM((clips, 3, rows, features), queries.dtype),
                pltpu.SemaphoreType.DMA((clips, 3)),
            ],
        ),
        out_shape=pltpu.HBM((heads, 3, clips, rows, HD), queries.dtype),
        compiler_params=pltpu.CompilerParams(vmem_limit_bytes=VMEM_LIMIT),
        name="pack",
    )(in_hbm(lengths), group, in_hbm(queries), in_hbm(keys), in_hbm(values))


def attend_head(head, count, q_ref, k_ref, v_ref, out_ref, scratch):
    values_ref, keys_ref, score_ref, max_ref, low_ref, high_ref, summed_ref = scratch
    rows_each = q_ref.shape[4]
    block_rows = score_ref.shape[1]
    half_rows = block_rows // 2
    pieces = block_rows // rows_each
    blocks = (count + block_rows - 1) // block_rows
    halves = [slice(0, half_rows), slice(half_rows, block_rows)]

    def score_block(query_rows, block, masked):
        for half in halves:
            scores = jnp.dot(query_rows[half], keys_ref[block], preferred_element_type=jnp.float32)
            if masked:
                columns = block * block_rows + lax.broadcasted_iota(jnp.int32, (1, block_rows), 1)
                scores = jnp.where(columns < count, scores, -jnp.inf)
            score_ref[block, half, :] = scores
            lane_max = scores[:, :HD]
            for start in range(HD, block_rows, HD):
                lane_max = jnp.maximum(lane_max, scores[:, start : start + HD])
            max_ref[half, :] = jnp.maximum(max_ref[half, :], lane_max)

    def weight_block(block, carry):
        value_rows = values_ref[pl.ds(pl.multiple_of(block * block_rows, block_rows), block_rows)]
        for half, weight_ref in zip(halves, (low_ref, high_ref)):
            for row in range(0, half_rows, PIECE):
                rows = slice(half.start + row, half.start + row + PIECE)
                row_max = max_ref[rows, :]
                for start in range(0, block_rows, HD):
                    scores = score_ref[block, rows, start : start + HD]
                    weights = jnp.exp2((scores - row_max) * EXP2_SCALE)
                    weight_ref[row : row + PIECE, start : start + HD] = weights.astype(weight_ref.dtype)
            summed_ref[half, :] += jnp.dot(weight_ref[...], value_rows, preferred_element_type=jnp.float32)
        return carry

    def tile(step, carry):
        at = pl.ds(step * pieces, pieces)
        query_rows = q_ref[at, head].reshape(block_rows, HD)
        max_ref[...] = jnp.full_like(max_ref, -jnp.inf)

        def whole_block(block, inner):
            score_block(query_rows, block, False)
            return inner

        lax.fori_loop(0, blocks - 1, whole_block, 0)
        score_block(query_rows, blocks - 1, True)
        max_ref[...] = jnp.broadcast_to(jnp.max(max_ref[...], axis=1, keepdims=True), max_ref.shape)
        summed_ref[...] = jnp.zeros_like(summed_ref)
        lax.fori_loop(0, blocks, weight_block, 0)
        rows = step * block_rows + lax.broadcasted_iota(jnp.int32, (block_rows, HD), 0)
        attended = jnp.where(rows < count, summed_ref[:, :HD] / summed_ref[:, HD:], 0.0)
        out_ref[at, head] = attended.astype(out_ref.dtype).reshape(pieces, 1, rows_each, HD)
        return carry

    def turn_block(block, carry):
        key_rows = k_ref[pl.ds(block * pieces, pieces), head].reshape(block_rows, HD)
        keys_ref[block] = key_rows.T
        return carry

    lax.fori_loop(0, blocks, turn_block, 0)
    values_ref[:, :HD] = v_ref[:, head].reshape(values_ref.shape[0], HD)
    lax.fori_loop(0, blocks, tile, 0)


def attend(lengths, group, place, first, clips, sources, per_group, arrived, into=None, out_clips=None):
    earlier = [] if into is None else [in_hbm(into)]
    out_first = 0 if into is None else first
    out_clips = out_clips or clips
    heads, rows = arrived.shape[0] // sources, arrived.shape[3]
    held_rows = sources * rows
    block_rows = min(BLOCK, held_rows)
    arrived = arrived.reshape(sources, heads, 3, clips, rows, HD)
    whole = lambda position: pl.BlockSpec(
        (sources, heads, 1, 1, rows, HD), lambda c, ln, gr, at: (0, 0, position, c, 0, 0)
    )

    def kernel(lengths_ref, group_ref, place_ref, q_ref, k_ref, v_ref, *refs):
        out_ref, *scratch = refs[len(earlier) :]
        count = by_length(lengths_ref, group_ref, per_group, first + pl.program_id(0))[1]
        count = jnp.where(place_ref[0] < sources, count, 0)
        out_ref[...] = jnp.zeros_like(out_ref)

        @pl.when(pl.program_id(0) == 0)
        def _():
            scratch[0][:, HD:] = jnp.ones((held_rows, HD), scratch[0].dtype)

        def by_head(head, carry):
            attend_head(head, count, q_ref, k_ref, v_ref, out_ref, scratch)
            return carry

        @pl.when(count > 0)
        def _():
            lax.fori_loop(0, heads, by_head, 0)

    attended = pl.pallas_call(
        kernel,
        grid_spec=pltpu.PrefetchScalarGridSpec(
            num_scalar_prefetch=3,
            grid=(clips,),
            in_specs=[whole(0), whole(1), whole(2)] + [pl.BlockSpec(memory_space=pl.ANY)] * len(earlier),
            out_specs=pl.BlockSpec(
                (sources, heads, 1, rows, HD), lambda c, ln, gr, at: (0, 0, c + out_first, 0, 0)
            ),
            scratch_shapes=[
                pltpu.VMEM((held_rows, 2 * HD), arrived.dtype),
                pltpu.VMEM((held_rows // block_rows, HD, block_rows), arrived.dtype),
                pltpu.VMEM((held_rows // block_rows, block_rows, block_rows), jnp.float32),
                pltpu.VMEM((block_rows, HD), jnp.float32),
                pltpu.VMEM((block_rows // 2, block_rows), arrived.dtype),
                pltpu.VMEM((block_rows // 2, block_rows), arrived.dtype),
                pltpu.VMEM((block_rows, 2 * HD), jnp.float32),
            ],
        ),
        out_shape=pltpu.HBM((sources, heads, out_clips, rows, HD), arrived.dtype),
        input_output_aliases={6: 0} if earlier else {},
        compiler_params=pltpu.CompilerParams(vmem_limit_bytes=VMEM_LIMIT),
        name="attend",
    )(in_hbm(lengths), group, place, arrived, arrived, arrived, *earlier)
    if out_clips != clips:
        return attended
    return attended.reshape(sources * heads, clips, rows, HD)


def unpack(lengths, group, parts, returned):
    heads, _, rows, _ = returned[0].shape
    per_group = sum(clips for _, clips, _ in parts)

    def kernel(lengths_ref, group_ref, *refs):
        out_ref = refs[-1]
        rank = pl.program_id(0)
        for (first, clips, _), in_ref in zip(parts, refs):

            @pl.when((rank >= first) & (rank < first + clips))
            def _(in_ref=in_ref):

                def by_head(head, carry):
                    out_ref[0, :, pl.ds(pl.multiple_of(head * HD, HD), HD)] = in_ref[head, 0]
                    return carry

                lax.fori_loop(0, heads, by_head, 0, unroll=4)

    return pl.pallas_call(
        kernel,
        grid_spec=pltpu.PrefetchScalarGridSpec(
            num_scalar_prefetch=2,
            grid=(per_group,),
            in_specs=[
                pl.BlockSpec(
                    (heads, 1, rows, HD),
                    lambda c, ln, gr, first=first, clips=clips: (0, jnp.clip(c - first, 0, clips - 1), 0, 0),
                )
                for first, clips, _ in parts
            ],
            out_specs=pl.BlockSpec(
                (1, rows, heads * HD), lambda c, ln, gr: (by_length(ln, gr, per_group, c)[0], 0, 0)
            ),
        ),
        out_shape=pltpu.HBM((per_group, rows, heads * HD), returned[0].dtype),
        compiler_params=pltpu.CompilerParams(vmem_limit_bytes=VMEM_LIMIT),
        name="unpack",
    )(in_hbm(lengths), group, *returned)


def exchange(array, peers):
    devices = lax.axis_size("seq")
    blocks = [list(range(start, start + peers)) for start in range(0, devices, peers)]
    return lax.all_to_all(
        array, "seq", split_axis=0, concat_axis=0, axis_index_groups=blocks, tiled=True
    )


def planned(parts, together=False):
    def run(queries, keys, values, lengths, group, place):
        per_group = queries.shape[0]
        arrived, before = [], None
        for first, clips, peers in parts:
            packed = pack(lengths, group, first, clips, queries, keys, values)
            if before is not None:
                packed, before = lax.optimization_barrier((packed, before))
                arrived[-1] = before
            before = exchange(packed, peers)
            arrived.append(before)
        if together:
            attended = None
            for (first, clips, peers), rows in zip(parts, arrived):
                attended = attend(
                    lengths, group, place, first, clips, peers, per_group, rows, attended, per_group
                )
            attended = attended.reshape(peers, per_group, *attended.shape[3:])
            return unpack(lengths, group, ((0, per_group, peers),), [exchange(attended, peers)])
        returned = []
        for (first, clips, peers), rows in zip(parts, arrived):
            attended = attend(lengths, group, place, first, clips, peers, per_group, rows)
            attended, before = lax.optimization_barrier((attended, before))
            before = exchange(attended, peers)
            returned.append(before)
        return unpack(lengths, group, parts, returned)

    return run


PLANS = (
    (((0, 4, NEAR),),),
    (((0, 2, NEAR), (2, 2, NEAREST)),),
    (((2, 2, NEAR), (0, 2, WIDE)),),
    (((0, 2, WIDE), (2, 2, NEAR)),),
    (((3, 1, NEAR), (0, 3, WIDE)),),
    (((0, 3, WIDE), (3, 1, NEAR)),),
    (((0, 3, WIDE), (3, 1, WIDE)), True),
    (((3, 1, WIDE), (0, 3, WIDE)),),
)


def local(queries, key_tokens, value_tokens, clip_lengths):
    per_group, rows = queries.shape[:2]
    group, place = lax.axis_index("grp"), lax.axis_index("seq")
    slots = jnp.arange(clip_lengths.shape[0], dtype=jnp.int32)
    is_long = clip_lengths > NEAR * rows
    own = slots // per_group == group
    neighbour = slots // per_group == group + 1 - 2 * (group % 2)
    long = jnp.sum((own & is_long).astype(jnp.int32))
    long_beside = jnp.sum((neighbour & is_long).astype(jnp.int32))
    tiny = jnp.sum((own & (clip_lengths <= NEAREST * rows)).astype(jnp.int32))
    most = long == per_group
    second = (group % 2 == 1) & jnp.where(
        most, long_beside == per_group, (long_beside > 0) & (long_beside < per_group)
    )
    with_long = 2 * jnp.maximum(long - 1, 1) + second.astype(jnp.int32)
    chosen = jnp.where(long > 0, with_long, jnp.where(tiny >= 2, 1, 0))
    return lax.switch(
        chosen,
        [planned(*plan) for plan in PLANS],
        queries, key_tokens, value_tokens, clip_lengths, group.reshape(1), place.reshape(1),
    )


def solution(mesh):
    in_specs = (P("grp", "seq", None), P("grp", "seq", None), P("grp", "seq", None), P())
    out_specs = P("grp", "seq", None)
    return jax.shard_map(local, mesh=mesh, in_specs=in_specs, out_specs=out_specs, check_vma=False)
```

```python
import jax
import jax.numpy as jnp
from jax import lax
from jax.experimental import pallas as pl
from jax.experimental.pallas import tpu as pltpu
from jax.sharding import PartitionSpec as P

HD = 128
EXP2_SCALE = HD ** (-0.5) * 1.4426950408889634
BLOCK = 512
PIECE = 64
WIDE, NEAR, NEAREST = 32, 8, 4
VMEM_LIMIT = 24 * 2**20


def in_hbm(array):
    return pltpu.with_memory_space_constraint(array, pltpu.HBM)


def by_length(lengths_ref, group_ref, per_group, rank):
    lengths = [lengths_ref[group_ref[0] * per_group + slot] for slot in range(per_group)]
    slot_at_rank, length_at_rank = jnp.int32(0), jnp.int32(0)
    for slot in range(per_group):
        place = jnp.int32(0)
        for other in range(per_group):
            if other < slot:
                place += (lengths[other] >= lengths[slot]).astype(jnp.int32)
            elif other > slot:
                place += (lengths[other] > lengths[slot]).astype(jnp.int32)
        slot_at_rank = jnp.where(place == rank, slot, slot_at_rank)
        length_at_rank = jnp.where(place == rank, lengths[slot], length_at_rank)
    return slot_at_rank, length_at_rank


def pack(lengths, group, first, clips, queries, keys, values):
    per_group, rows, features = queries.shape
    heads = features // HD

    def kernel(lengths_ref, group_ref, q_ref, k_ref, v_ref, out_ref, held, sems):
        def fetch(clip, position):
            slot = by_length(lengths_ref, group_ref, per_group, first + clip)[0]
            source = (q_ref, k_ref, v_ref)[position].at[slot]
            return pltpu.make_async_copy(source, held.at[clip, position], sems.at[clip, position])

        clip = pl.program_id(0)

        @pl.when(clip == 0)
        def _():
            for each in range(clips):
                for position in range(3):
                    fetch(each, position).start()

        for position in range(3):
            fetch(clip, position).wait()

        def by_head(head, carry):
            columns = pl.ds(pl.multiple_of(head * HD, HD), HD)
            for position in range(3):
                out_ref[head, position, 0] = held[clip, position, :, columns]
            return carry

        lax.fori_loop(0, heads, by_head, 0, unroll=4)

    return pl.pallas_call(
        kernel,
        grid_spec=pltpu.PrefetchScalarGridSpec(
            num_scalar_prefetch=2,
            grid=(clips,),
            in_specs=[pl.BlockSpec(memory_space=pltpu.HBM)] * 3,
            out_specs=pl.BlockSpec((heads, 3, 1, rows, HD), lambda c, ln, gr: (0, 0, c, 0, 0)),
            scratch_shapes=[
                pltpu.VMEM((clips, 3, rows, features), queries.dtype),
                pltpu.SemaphoreType.DMA((clips, 3)),
            ],
        ),
        out_shape=pltpu.HBM((heads, 3, clips, rows, HD), queries.dtype),
        compiler_params=pltpu.CompilerParams(vmem_limit_bytes=VMEM_LIMIT),
        name="pack",
    )(in_hbm(lengths), group, in_hbm(queries), in_hbm(keys), in_hbm(values))


def attend_head(head, count, q_ref, k_ref, v_ref, out_ref, scratch):
    values_ref, keys_ref, score_ref, max_ref, weight_ref, summed_ref = scratch
    rows_each = q_ref.shape[4]
    block_rows = score_ref.shape[1]
    pieces = block_rows // rows_each
    blocks = (count + block_rows - 1) // block_rows

    def score_block(query_rows, block, masked):
        scores = jnp.dot(query_rows, keys_ref[block], preferred_element_type=jnp.float32)
        if masked:
            columns = block * block_rows + lax.broadcasted_iota(jnp.int32, (1, block_rows), 1)
            scores = jnp.where(columns < count, scores, -jnp.inf)
        score_ref[block] = scores
        lane_max = scores[:, :HD]
        for start in range(HD, block_rows, HD):
            lane_max = jnp.maximum(lane_max, scores[:, start : start + HD])
        max_ref[...] = jnp.maximum(max_ref[...], lane_max)

    def weight_block(block, carry):
        value_rows = values_ref[pl.ds(pl.multiple_of(block * block_rows, block_rows), block_rows)]
        for row in range(0, block_rows, PIECE):
            rows = slice(row, row + PIECE)
            row_max = max_ref[rows, :]
            for start in range(0, block_rows, HD):
                scores = score_ref[block, rows, start : start + HD]
                weights = jnp.exp2((scores - row_max) * EXP2_SCALE)
                weight_ref[rows, start : start + HD] = weights.astype(weight_ref.dtype)
        summed_ref[...] += jnp.dot(weight_ref[...], value_rows, preferred_element_type=jnp.float32)
        return carry

    def tile(step, carry):
        at = pl.ds(step * pieces, pieces)
        query_rows = q_ref[at, head].reshape(block_rows, HD)
        max_ref[...] = jnp.full_like(max_ref, -jnp.inf)

        def whole_block(block, inner):
            score_block(query_rows, block, False)
            return inner

        lax.fori_loop(0, blocks - 1, whole_block, 0)
        score_block(query_rows, blocks - 1, True)
        max_ref[...] = jnp.broadcast_to(jnp.max(max_ref[...], axis=1, keepdims=True), max_ref.shape)
        summed_ref[...] = jnp.zeros_like(summed_ref)
        lax.fori_loop(0, blocks, weight_block, 0)
        rows = step * block_rows + lax.broadcasted_iota(jnp.int32, (block_rows, HD), 0)
        attended = jnp.where(rows < count, summed_ref[:, :HD] / summed_ref[:, HD:], 0.0)
        out_ref[at, head] = attended.astype(out_ref.dtype).reshape(pieces, 1, rows_each, HD)
        return carry

    def turn_block(block, carry):
        key_rows = k_ref[pl.ds(block * pieces, pieces), head].reshape(block_rows, HD)
        keys_ref[block] = key_rows.T
        return carry

    lax.fori_loop(0, blocks, turn_block, 0)
    values_ref[:, :HD] = v_ref[:, head].reshape(values_ref.shape[0], HD)
    lax.fori_loop(0, blocks, tile, 0)


def attend(lengths, group, place, first, clips, sources, per_group, arrived, into=None, out_clips=None):
    earlier = [] if into is None else [in_hbm(into)]
    out_first = 0 if into is None else first
    out_clips = out_clips or clips
    heads, rows = arrived.shape[0] // sources, arrived.shape[3]
    held_rows = sources * rows
    block_rows = min(BLOCK, held_rows)
    arrived = arrived.reshape(sources, heads, 3, clips, rows, HD)
    whole = lambda position: pl.BlockSpec(
        (sources, heads, 1, 1, rows, HD), lambda c, ln, gr, at: (0, 0, position, c, 0, 0)
    )

    def kernel(lengths_ref, group_ref, place_ref, q_ref, k_ref, v_ref, *refs):
        out_ref, *scratch = refs[len(earlier) :]
        count = by_length(lengths_ref, group_ref, per_group, first + pl.program_id(0))[1]
        count = jnp.where(place_ref[0] < sources, count, 0)
        out_ref[...] = jnp.zeros_like(out_ref)

        @pl.when(pl.program_id(0) == 0)
        def _():
            scratch[0][:, HD:] = jnp.ones((held_rows, HD), scratch[0].dtype)

        def by_head(head, carry):
            attend_head(head, count, q_ref, k_ref, v_ref, out_ref, scratch)
            return carry

        @pl.when(count > 0)
        def _():
            lax.fori_loop(0, heads, by_head, 0)

    attended = pl.pallas_call(
        kernel,
        grid_spec=pltpu.PrefetchScalarGridSpec(
            num_scalar_prefetch=3,
            grid=(clips,),
            in_specs=[whole(0), whole(1), whole(2)] + [pl.BlockSpec(memory_space=pl.ANY)] * len(earlier),
            out_specs=pl.BlockSpec(
                (sources, heads, 1, rows, HD), lambda c, ln, gr, at: (0, 0, c + out_first, 0, 0)
            ),
            scratch_shapes=[
                pltpu.VMEM((held_rows, 2 * HD), arrived.dtype),
                pltpu.VMEM((held_rows // block_rows, HD, block_rows), arrived.dtype),
                pltpu.VMEM((held_rows // block_rows, block_rows, block_rows), jnp.float32),
                pltpu.VMEM((block_rows, HD), jnp.float32),
                pltpu.VMEM((block_rows, block_rows), arrived.dtype),
                pltpu.VMEM((block_rows, 2 * HD), jnp.float32),
            ],
        ),
        out_shape=pltpu.HBM((sources, heads, out_clips, rows, HD), arrived.dtype),
        input_output_aliases={6: 0} if earlier else {},
        compiler_params=pltpu.CompilerParams(vmem_limit_bytes=VMEM_LIMIT),
        name="attend",
    )(in_hbm(lengths), group, place, arrived, arrived, arrived, *earlier)
    if out_clips != clips:
        return attended
    return attended.reshape(sources * heads, clips, rows, HD)


def unpack(lengths, group, parts, returned):
    heads, _, rows, _ = returned[0].shape
    per_group = sum(clips for _, clips, _ in parts)

    def kernel(lengths_ref, group_ref, *refs):
        out_ref = refs[-1]
        rank = pl.program_id(0)
        for (first, clips, _), in_ref in zip(parts, refs):

            @pl.when((rank >= first) & (rank < first + clips))
            def _(in_ref=in_ref):

                def by_head(head, carry):
                    out_ref[0, :, pl.ds(pl.multiple_of(head * HD, HD), HD)] = in_ref[head, 0]
                    return carry

                lax.fori_loop(0, heads, by_head, 0, unroll=4)

    return pl.pallas_call(
        kernel,
        grid_spec=pltpu.PrefetchScalarGridSpec(
            num_scalar_prefetch=2,
            grid=(per_group,),
            in_specs=[
                pl.BlockSpec(
                    (heads, 1, rows, HD),
                    lambda c, ln, gr, first=first, clips=clips: (0, jnp.clip(c - first, 0, clips - 1), 0, 0),
                )
                for first, clips, _ in parts
            ],
            out_specs=pl.BlockSpec(
                (1, rows, heads * HD), lambda c, ln, gr: (by_length(ln, gr, per_group, c)[0], 0, 0)
            ),
        ),
        out_shape=pltpu.HBM((per_group, rows, heads * HD), returned[0].dtype),
        compiler_params=pltpu.CompilerParams(vmem_limit_bytes=VMEM_LIMIT),
        name="unpack",
    )(in_hbm(lengths), group, *returned)


def exchange(array, peers):
    devices = lax.axis_size("seq")
    blocks = [list(range(start, start + peers)) for start in range(0, devices, peers)]
    return lax.all_to_all(
        array, "seq", split_axis=0, concat_axis=0, axis_index_groups=blocks, tiled=True
    )


def planned(parts, together=False):
    def run(queries, keys, values, lengths, group, place):
        per_group = queries.shape[0]
        arrived, before = [], None
        for first, clips, peers in parts:
            packed = pack(lengths, group, first, clips, queries, keys, values)
            if before is not None:
                packed, before = lax.optimization_barrier((packed, before))
                arrived[-1] = before
            before = exchange(packed, peers)
            arrived.append(before)
        if together:
            attended = None
            for (first, clips, peers), rows in zip(parts, arrived):
                attended = attend(
                    lengths, group, place, first, clips, peers, per_group, rows, attended, per_group
                )
            attended = attended.reshape(peers, per_group, *attended.shape[3:])
            return unpack(lengths, group, ((0, per_group, peers),), [exchange(attended, peers)])
        returned = []
        for (first, clips, peers), rows in zip(parts, arrived):
            attended = attend(lengths, group, place, first, clips, peers, per_group, rows)
            attended, before = lax.optimization_barrier((attended, before))
            before = exchange(attended, peers)
            returned.append(before)
        return unpack(lengths, group, parts, returned)

    return run


PLANS = (
    (((0, 4, NEAR),),),
    (((0, 2, NEAR), (2, 2, NEAREST)),),
    (((2, 2, NEAR), (0, 2, WIDE)),),
    (((0, 2, WIDE), (2, 2, NEAR)),),
    (((3, 1, NEAR), (0, 3, WIDE)),),
    (((0, 3, WIDE), (3, 1, NEAR)),),
    (((0, 3, WIDE), (3, 1, WIDE)), True),
    (((3, 1, WIDE), (0, 3, WIDE)),),
)


def choose_plan(lengths, group, per_group, rows):
    def kernel(lengths_ref, group_ref, out_ref):
        mine = group_ref[0]
        odd = lax.rem(mine, 2)

        def how_many(which, test):
            return sum(
                test(lengths_ref[which * per_group + slot]).astype(jnp.int32) for slot in range(per_group)
            )

        long = how_many(mine, lambda length: length > NEAR * rows)
        tiny = how_many(mine, lambda length: length <= NEAREST * rows)
        beside = how_many(mine + 1 - 2 * odd, lambda length: length > NEAR * rows)
        differ = jnp.where(
            long == per_group, beside == per_group, (beside > 0) & (beside < per_group)
        )
        with_long = 2 * jnp.maximum(long - 1, 1) + odd * differ.astype(jnp.int32)
        out_ref[0] = jnp.where(long > 0, with_long, (tiny >= 2).astype(jnp.int32))

    return pl.pallas_call(
        kernel,
        grid_spec=pltpu.PrefetchScalarGridSpec(
            num_scalar_prefetch=2,
            grid=(),
            in_specs=[],
            out_specs=pl.BlockSpec(memory_space=pltpu.SMEM),
        ),
        out_shape=jax.ShapeDtypeStruct((1,), jnp.int32),
        name="choose_plan",
    )(in_hbm(lengths), group)


def local(queries, key_tokens, value_tokens, clip_lengths):
    per_group, rows = queries.shape[:2]
    group, place = lax.axis_index("grp").reshape(1), lax.axis_index("seq").reshape(1)
    return lax.switch(
        choose_plan(clip_lengths, group, per_group, rows)[0],
        [planned(*plan) for plan in PLANS],
        queries, key_tokens, value_tokens, clip_lengths, group, place,
    )


def solution(mesh):
    in_specs = (P("grp", "seq", None), P("grp", "seq", None), P("grp", "seq", None), P())
    out_specs = P("grp", "seq", None)
    return jax.shard_map(local, mesh=mesh, in_specs=in_specs, out_specs=out_specs, check_vma=False)
```

```python
import jax
import jax.numpy as jnp
from jax import lax
from jax.experimental import pallas as pl
from jax.experimental.pallas import tpu as pltpu
from jax.sharding import PartitionSpec as P

HD = 128
EXP2_SCALE = HD ** (-0.5) * 1.4426950408889634
BLOCK = 512
PIECE = 64
UNROLL = 4
WIDE, NEAR, NEAREST = 32, 8, 4
VMEM_LIMIT = 24 * 2**20


def in_hbm(array):
    return pltpu.with_memory_space_constraint(array, pltpu.HBM)


def by_length(lengths_ref, group_ref, per_group, rank):
    lengths = [lengths_ref[group_ref[0] * per_group + slot] for slot in range(per_group)]
    slot_at_rank, length_at_rank = jnp.int32(0), jnp.int32(0)
    for slot in range(per_group):
        place = jnp.int32(0)
        for other in range(per_group):
            if other < slot:
                place += (lengths[other] >= lengths[slot]).astype(jnp.int32)
            elif other > slot:
                place += (lengths[other] > lengths[slot]).astype(jnp.int32)
        slot_at_rank = jnp.where(place == rank, slot, slot_at_rank)
        length_at_rank = jnp.where(place == rank, lengths[slot], length_at_rank)
    return slot_at_rank, length_at_rank


def pack(lengths, group, first, clips, queries, keys, values):
    per_group, rows, features = queries.shape
    heads = features // HD

    def kernel(lengths_ref, group_ref, q_ref, k_ref, v_ref, out_ref, held, sems):
        def fetch(clip, slot, position):
            source = (q_ref, k_ref, v_ref)[position].at[slot]
            return pltpu.make_async_copy(source, held.at[clip, position], sems.at[clip, position])

        clip = pl.program_id(0)

        @pl.when(clip == 0)
        def _():
            for each in range(clips):
                slot = by_length(lengths_ref, group_ref, per_group, first + each)[0]
                for position in range(3):
                    fetch(each, slot, position).start()

        for position in range(3):
            fetch(clip, 0, position).wait()

        def by_head(head, carry):
            columns = pl.ds(pl.multiple_of(head * HD, HD), HD)
            for position in range(3):
                out_ref[head, position, 0] = held[clip, position, :, columns]
            return carry

        lax.fori_loop(0, heads, by_head, 0, unroll=UNROLL)

    return pl.pallas_call(
        kernel,
        grid_spec=pltpu.PrefetchScalarGridSpec(
            num_scalar_prefetch=2,
            grid=(clips,),
            in_specs=[pl.BlockSpec(memory_space=pltpu.HBM)] * 3,
            out_specs=pl.BlockSpec((heads, 3, 1, rows, HD), lambda c, ln, gr: (0, 0, c, 0, 0)),
            scratch_shapes=[
                pltpu.VMEM((clips, 3, rows, features), queries.dtype),
                pltpu.SemaphoreType.DMA((clips, 3)),
            ],
        ),
        out_shape=pltpu.HBM((heads, 3, clips, rows, HD), queries.dtype),
        compiler_params=pltpu.CompilerParams(vmem_limit_bytes=VMEM_LIMIT),
        name="pack",
    )(in_hbm(lengths), group, in_hbm(queries), in_hbm(keys), in_hbm(values))


def attend_head(head, count, q_ref, k_ref, v_ref, out_ref, scratch):
    values_ref, keys_ref, score_ref, max_ref, weight_ref, summed_ref = scratch
    rows_each = q_ref.shape[4]
    block_rows = score_ref.shape[1]
    pieces = block_rows // rows_each
    blocks = (count + block_rows - 1) // block_rows

    def score_block(query_rows, block, masked):
        scores = jnp.dot(query_rows, keys_ref[block], preferred_element_type=jnp.float32)
        if masked:
            columns = block * block_rows + lax.broadcasted_iota(jnp.int32, (1, block_rows), 1)
            scores = jnp.where(columns < count, scores, -jnp.inf)
        score_ref[block] = scores
        lane_max = scores[:, :HD]
        for start in range(HD, block_rows, HD):
            lane_max = jnp.maximum(lane_max, scores[:, start : start + HD])
        max_ref[...] = jnp.maximum(max_ref[...], lane_max)

    def weight_block(block, carry):
        value_rows = values_ref[pl.ds(pl.multiple_of(block * block_rows, block_rows), block_rows)]
        for row in range(0, block_rows, PIECE):
            rows = slice(row, row + PIECE)
            row_max = max_ref[rows, :]
            for start in range(0, block_rows, HD):
                scores = score_ref[block, rows, start : start + HD]
                weights = jnp.exp2((scores - row_max) * EXP2_SCALE)
                weight_ref[rows, start : start + HD] = weights.astype(weight_ref.dtype)
        summed_ref[...] += jnp.dot(weight_ref[...], value_rows, preferred_element_type=jnp.float32)
        return carry

    def tile(step, carry):
        at = pl.ds(step * pieces, pieces)
        query_rows = q_ref[at, head].reshape(block_rows, HD)
        max_ref[...] = jnp.full_like(max_ref, -jnp.inf)

        def whole_block(block, inner):
            score_block(query_rows, block, False)
            return inner

        lax.fori_loop(0, blocks - 1, whole_block, 0)
        score_block(query_rows, blocks - 1, True)
        max_ref[...] = jnp.broadcast_to(jnp.max(max_ref[...], axis=1, keepdims=True), max_ref.shape)
        summed_ref[...] = jnp.zeros_like(summed_ref)
        lax.fori_loop(0, blocks, weight_block, 0)
        rows = step * block_rows + lax.broadcasted_iota(jnp.int32, (block_rows, HD), 0)
        attended = jnp.where(rows < count, summed_ref[:, :HD] / summed_ref[:, HD:], 0.0)
        out_ref[at, head] = attended.astype(out_ref.dtype).reshape(pieces, 1, rows_each, HD)
        return carry

    def turn_block(block, carry):
        key_rows = k_ref[pl.ds(block * pieces, pieces), head].reshape(block_rows, HD)
        keys_ref[block] = key_rows.T
        return carry

    lax.fori_loop(0, blocks, turn_block, 0)
    values_ref[:, :HD] = v_ref[:, head].reshape(values_ref.shape[0], HD)
    lax.fori_loop(0, blocks, tile, 0)


def attend(lengths, group, place, first, clips, sources, per_group, arrived, into, out_first, out_clips):
    earlier = [] if into is None else [in_hbm(into)]
    heads, rows = arrived.shape[0] // sources, arrived.shape[3]
    held_rows = sources * rows
    block_rows = min(BLOCK, held_rows)
    arrived = arrived.reshape(sources, heads, 3, clips, rows, HD)
    whole = lambda position: pl.BlockSpec(
        (sources, heads, 1, 1, rows, HD), lambda c, ln, gr, at: (0, 0, position, c, 0, 0)
    )

    def kernel(lengths_ref, group_ref, place_ref, q_ref, k_ref, v_ref, *refs):
        out_ref, *scratch = refs[len(earlier) :]
        count = by_length(lengths_ref, group_ref, per_group, first + pl.program_id(0))[1]
        count = jnp.where(place_ref[0] < sources, count, 0)
        out_ref[...] = jnp.zeros_like(out_ref)

        @pl.when(pl.program_id(0) == 0)
        def _():
            scratch[0][:, HD:] = jnp.ones((held_rows, HD), scratch[0].dtype)

        def by_head(head, carry):
            attend_head(head, count, q_ref, k_ref, v_ref, out_ref, scratch)
            return carry

        @pl.when(count > 0)
        def _():
            lax.fori_loop(0, heads, by_head, 0)

    attended = pl.pallas_call(
        kernel,
        grid_spec=pltpu.PrefetchScalarGridSpec(
            num_scalar_prefetch=3,
            grid=(clips,),
            in_specs=[whole(0), whole(1), whole(2)] + [pl.BlockSpec(memory_space=pl.ANY)] * len(earlier),
            out_specs=pl.BlockSpec(
                (sources, heads, 1, rows, HD), lambda c, ln, gr, at: (0, 0, c + out_first, 0, 0)
            ),
            scratch_shapes=[
                pltpu.VMEM((held_rows, 2 * HD), arrived.dtype),
                pltpu.VMEM((held_rows // block_rows, HD, block_rows), arrived.dtype),
                pltpu.VMEM((held_rows // block_rows, block_rows, block_rows), jnp.float32),
                pltpu.VMEM((block_rows, HD), jnp.float32),
                pltpu.VMEM((block_rows, block_rows), arrived.dtype),
                pltpu.VMEM((block_rows, 2 * HD), jnp.float32),
            ],
        ),
        out_shape=pltpu.HBM((sources, heads, out_clips, rows, HD), arrived.dtype),
        input_output_aliases={6: 0} if earlier else {},
        compiler_params=pltpu.CompilerParams(vmem_limit_bytes=VMEM_LIMIT),
        name="attend",
    )(in_hbm(lengths), group, place, arrived, arrived, arrived, *earlier)
    return attended


def unpack(lengths, group, parts, returned):
    heads, _, rows, _ = returned[0].shape
    per_group = sum(clips for _, clips in parts)

    def kernel(lengths_ref, group_ref, *refs):
        out_ref = refs[-1]
        rank = pl.program_id(0)
        for (first, clips), in_ref in zip(parts, refs):

            @pl.when((rank >= first) & (rank < first + clips))
            def _(in_ref=in_ref):
                def by_head(head, carry):
                    out_ref[0, :, pl.ds(pl.multiple_of(head * HD, HD), HD)] = in_ref[head, 0]
                    return carry

                lax.fori_loop(0, heads, by_head, 0, unroll=UNROLL)

    return pl.pallas_call(
        kernel,
        grid_spec=pltpu.PrefetchScalarGridSpec(
            num_scalar_prefetch=2,
            grid=(per_group,),
            in_specs=[
                pl.BlockSpec(
                    (heads, 1, rows, HD),
                    lambda c, ln, gr, first=first, clips=clips: (0, jnp.clip(c - first, 0, clips - 1), 0, 0),
                )
                for first, clips in parts
            ],
            out_specs=pl.BlockSpec(
                (1, rows, heads * HD), lambda c, ln, gr: (by_length(ln, gr, per_group, c)[0], 0, 0)
            ),
        ),
        out_shape=pltpu.HBM((per_group, rows, heads * HD), returned[0].dtype),
        compiler_params=pltpu.CompilerParams(vmem_limit_bytes=VMEM_LIMIT),
        name="unpack",
    )(in_hbm(lengths), group, *returned)


def exchange(array, peers):
    devices = lax.axis_size("seq")
    blocks = [list(range(start, start + peers)) for start in range(0, devices, peers)]
    return lax.all_to_all(
        array, "seq", split_axis=0, concat_axis=0, axis_index_groups=blocks, tiled=True
    )


def planned(*outputs, order):
    def run(queries, keys, values, lengths, group, place):
        per_group = queries.shape[0]
        arrived, before = {}, None
        for part in order:
            packed = pack(lengths, group, part[0], part[1], queries, keys, values)
            if before is not None:
                packed, arrived[before] = lax.optimization_barrier((packed, arrived[before]))
            arrived[part] = exchange(packed, part[2])
            before = part
        last = arrived[before]
        attended, places = [], []
        for output in outputs:
            first, total = output[0][0], sum(part[1] for part in output)
            places.append((first, total))
            results = None
            for part in output:
                if part != before:
                    results = attend(
                        lengths, group, place, *part, per_group, arrived[part], results, part[0] - first, total
                    )
            attended.append(results)
        attended, last = lax.optimization_barrier((attended, last))
        returned = []
        for output, (first, total), results in zip(outputs, places, attended):
            part, peers = output[-1], output[-1][2]
            if part == before:
                results = attend(
                    lengths, group, place, *part, per_group, arrived[part], results, part[0] - first, total
                )
            results = results.reshape(-1, *results.shape[2:])
            results, last = lax.optimization_barrier((results, last))
            last = exchange(results, peers)
            returned.append(last)
        return unpack(lengths, group, places, returned)

    return run


FOUR, PAIR, TINY_PAIR = (0, 4, NEAR), (0, 2, NEAR), (2, 2, NEAREST)
TWO, ONE, THREE, LAST = (0, 2, WIDE), (2, 1, WIDE), (0, 3, WIDE), (3, 1, WIDE)
LAST_PAIR, SHORT, TINY = (2, 2, NEAR), (3, 1, NEAR), (3, 1, NEAREST)
PLANS = [
    planned([FOUR], order=[FOUR]),
    planned([TINY_PAIR], [PAIR], order=[TINY_PAIR, PAIR]),
    planned([LAST_PAIR], [TWO], order=[LAST_PAIR, TWO]),
    planned([TWO], [LAST_PAIR], order=[TWO, LAST_PAIR]),
    planned([SHORT], [TWO, ONE], order=[SHORT, TWO, ONE]),
    planned([THREE], [SHORT], order=[THREE, SHORT]),
    planned([THREE, LAST], order=[THREE, LAST]),
    planned([LAST], [THREE], order=[LAST, THREE]),
    planned([TINY], [TWO, ONE], order=[TINY, TWO, ONE]),
]


def choose_plan(lengths, group, per_group, rows):
    def kernel(lengths_ref, group_ref, out_ref):
        mine = group_ref[0]
        odd = lax.rem(mine, 2)

        def how_many(which, test):
            return sum(
                test(lengths_ref[which * per_group + slot]).astype(jnp.int32) for slot in range(per_group)
            )

        long = how_many(mine, lambda length: length > NEAR * rows)
        tiny = how_many(mine, lambda length: length <= NEAREST * rows)
        beside = how_many(mine + 1 - 2 * odd, lambda length: length > NEAR * rows)
        differ = jnp.where(
            long == per_group, beside == per_group, (beside > 0) & (beside < per_group)
        )
        with_long = 2 * jnp.maximum(long - 1, 1) + odd * differ.astype(jnp.int32)
        with_long = jnp.where((with_long == 4) & (tiny == 1), len(PLANS) - 1, with_long)
        out_ref[0] = jnp.where(long > 0, with_long, (tiny >= 2).astype(jnp.int32))

    return pl.pallas_call(
        kernel,
        grid_spec=pltpu.PrefetchScalarGridSpec(
            num_scalar_prefetch=2,
            grid=(),
            in_specs=[],
            out_specs=pl.BlockSpec(memory_space=pltpu.SMEM),
        ),
        out_shape=jax.ShapeDtypeStruct((1,), jnp.int32),
        name="choose_plan",
    )(in_hbm(lengths), group)


def local(queries, key_tokens, value_tokens, clip_lengths):
    per_group, rows = queries.shape[:2]
    group, place = lax.axis_index("grp").reshape(1), lax.axis_index("seq").reshape(1)
    return lax.switch(
        choose_plan(clip_lengths, group, per_group, rows)[0],
        PLANS,
        queries, key_tokens, value_tokens, clip_lengths, group, place,
    )


def solution(mesh):
    in_specs = (P("grp", "seq", None), P("grp", "seq", None), P("grp", "seq", None), P())
    out_specs = P("grp", "seq", None)
    return jax.shard_map(local, mesh=mesh, in_specs=in_specs, out_specs=out_specs, check_vma=False)
```

```python
import jax
import jax.numpy as jnp
from jax import lax
from jax.experimental import pallas as pl
from jax.experimental.pallas import tpu as pltpu
from jax.sharding import PartitionSpec as P

HD = 128
EXP2_SCALE = HD ** (-0.5) * 1.4426950408889634
BLOCK = 512
PIECE = 64
UNROLL = 4
WIDE, NEAR, NEAREST = 32, 8, 4
VMEM_LIMIT = 24 * 2**20


def in_hbm(array):
    return pltpu.with_memory_space_constraint(array, pltpu.HBM)


def by_length(lengths_ref, group_ref, per_group, rank):
    lengths = [lengths_ref[group_ref[0] * per_group + slot] for slot in range(per_group)]
    slot_at_rank, length_at_rank = jnp.int32(0), jnp.int32(0)
    for slot in range(per_group):
        place = jnp.int32(0)
        for other in range(per_group):
            if other < slot:
                place += (lengths[other] >= lengths[slot]).astype(jnp.int32)
            elif other > slot:
                place += (lengths[other] > lengths[slot]).astype(jnp.int32)
        slot_at_rank = jnp.where(place == rank, slot, slot_at_rank)
        length_at_rank = jnp.where(place == rank, lengths[slot], length_at_rank)
    return slot_at_rank, length_at_rank


def pack(lengths, group, first, clips, queries, keys, values):
    per_group, rows, features = queries.shape
    heads = features // HD

    def kernel(lengths_ref, group_ref, q_ref, k_ref, v_ref, out_ref, held, sems):
        def fetch(clip, slot, position):
            source = (q_ref, k_ref, v_ref)[position].at[slot]
            return pltpu.make_async_copy(source, held.at[clip, position], sems.at[clip, position])

        clip = pl.program_id(0)

        @pl.when(clip == 0)
        def _():
            for each in range(clips):
                slot = by_length(lengths_ref, group_ref, per_group, first + each)[0]
                for position in range(3):
                    fetch(each, slot, position).start()

        for position in range(3):
            fetch(clip, 0, position).wait()

        def by_head(head, carry):
            columns = pl.ds(pl.multiple_of(head * HD, HD), HD)
            for position in range(3):
                out_ref[head, position, 0] = held[clip, position, :, columns]
            return carry

        lax.fori_loop(0, heads, by_head, 0, unroll=UNROLL)

    return pl.pallas_call(
        kernel,
        grid_spec=pltpu.PrefetchScalarGridSpec(
            num_scalar_prefetch=2,
            grid=(clips,),
            in_specs=[pl.BlockSpec(memory_space=pltpu.HBM)] * 3,
            out_specs=pl.BlockSpec((heads, 3, 1, rows, HD), lambda c, ln, gr: (0, 0, c, 0, 0)),
            scratch_shapes=[
                pltpu.VMEM((clips, 3, rows, features), queries.dtype),
                pltpu.SemaphoreType.DMA((clips, 3)),
            ],
        ),
        out_shape=pltpu.HBM((heads, 3, clips, rows, HD), queries.dtype),
        compiler_params=pltpu.CompilerParams(vmem_limit_bytes=VMEM_LIMIT),
        name="pack",
    )(in_hbm(lengths), group, in_hbm(queries), in_hbm(keys), in_hbm(values))


def attend_head(head, count, q_ref, k_ref, v_ref, out_ref, scratch):
    values_ref, keys_ref, score_ref, max_ref, weight_ref, summed_ref = scratch
    rows_each = q_ref.shape[4]
    block_rows = score_ref.shape[1]
    pieces = block_rows // rows_each
    blocks = (count + block_rows - 1) // block_rows

    def score_block(query_rows, block, masked):
        scores = jnp.dot(query_rows, keys_ref[block], preferred_element_type=jnp.float32)
        if masked:
            columns = block * block_rows + lax.broadcasted_iota(jnp.int32, (1, block_rows), 1)
            scores = jnp.where(columns < count, scores, -jnp.inf)
        score_ref[block] = scores
        lane_max = scores[:, :HD]
        for start in range(HD, block_rows, HD):
            lane_max = jnp.maximum(lane_max, scores[:, start : start + HD])
        max_ref[...] = jnp.maximum(max_ref[...], lane_max)

    def weight_block(block, carry):
        value_rows = values_ref[pl.ds(pl.multiple_of(block * block_rows, block_rows), block_rows)]
        for row in range(0, block_rows, PIECE):
            rows = slice(row, row + PIECE)
            row_max = max_ref[rows, :]
            for start in range(0, block_rows, HD):
                scores = score_ref[block, rows, start : start + HD]
                weights = jnp.exp2((scores - row_max) * EXP2_SCALE)
                weight_ref[rows, start : start + HD] = weights.astype(weight_ref.dtype)
        summed_ref[...] += jnp.dot(weight_ref[...], value_rows, preferred_element_type=jnp.float32)
        return carry

    def tile(step, carry):
        at = pl.ds(step * pieces, pieces)
        query_rows = q_ref[at, head].reshape(block_rows, HD)
        max_ref[...] = jnp.full_like(max_ref, -jnp.inf)

        def whole_block(block, inner):
            score_block(query_rows, block, False)
            return inner

        lax.fori_loop(0, blocks - 1, whole_block, 0)
        score_block(query_rows, blocks - 1, True)
        max_ref[...] = jnp.broadcast_to(jnp.max(max_ref[...], axis=1, keepdims=True), max_ref.shape)
        summed_ref[...] = jnp.zeros_like(summed_ref)
        lax.fori_loop(0, blocks, weight_block, 0)
        rows = step * block_rows + lax.broadcasted_iota(jnp.int32, (block_rows, HD), 0)
        attended = jnp.where(rows < count, summed_ref[:, :HD] / summed_ref[:, HD:], 0.0)
        out_ref[at, head] = attended.astype(out_ref.dtype).reshape(pieces, 1, rows_each, HD)
        return carry

    def turn_block(block, carry):
        key_rows = k_ref[pl.ds(block * pieces, pieces), head].reshape(block_rows, HD)
        keys_ref[block] = key_rows.T
        return carry

    lax.fori_loop(0, blocks, turn_block, 0)
    values_ref[:, :HD] = v_ref[:, head].reshape(values_ref.shape[0], HD)
    lax.fori_loop(0, blocks, tile, 0)


def attend(lengths, group, place, first, clips, sources, per_group, arrived, into, out_first, out_clips):
    earlier = [] if into is None else [in_hbm(into)]
    heads, rows = arrived.shape[0] // sources, arrived.shape[3]
    held_rows = sources * rows
    block_rows = min(BLOCK, held_rows)
    arrived = arrived.reshape(sources, heads, 3, clips, rows, HD)
    whole = lambda position: pl.BlockSpec(
        (sources, heads, 1, 1, rows, HD), lambda c, ln, gr, at: (0, 0, position, c, 0, 0)
    )

    def kernel(lengths_ref, group_ref, place_ref, q_ref, k_ref, v_ref, *refs):
        out_ref, *scratch = refs[len(earlier) :]
        count = by_length(lengths_ref, group_ref, per_group, first + pl.program_id(0))[1]
        count = jnp.where(place_ref[0] < sources, count, 0)
        out_ref[...] = jnp.zeros_like(out_ref)

        @pl.when(pl.program_id(0) == 0)
        def _():
            scratch[0][:, HD:] = jnp.ones((held_rows, HD), scratch[0].dtype)

        def by_head(head, carry):
            attend_head(head, count, q_ref, k_ref, v_ref, out_ref, scratch)
            return carry

        @pl.when(count > 0)
        def _():
            lax.fori_loop(0, heads, by_head, 0)

    attended = pl.pallas_call(
        kernel,
        grid_spec=pltpu.PrefetchScalarGridSpec(
            num_scalar_prefetch=3,
            grid=(clips,),
            in_specs=[whole(0), whole(1), whole(2)] + [pl.BlockSpec(memory_space=pl.ANY)] * len(earlier),
            out_specs=pl.BlockSpec(
                (sources, heads, 1, rows, HD), lambda c, ln, gr, at: (0, 0, c + out_first, 0, 0)
            ),
            scratch_shapes=[
                pltpu.VMEM((held_rows, 2 * HD), arrived.dtype),
                pltpu.VMEM((held_rows // block_rows, HD, block_rows), arrived.dtype),
                pltpu.VMEM((held_rows // block_rows, block_rows, block_rows), jnp.float32),
                pltpu.VMEM((block_rows, HD), jnp.float32),
                pltpu.VMEM((block_rows, block_rows), arrived.dtype),
                pltpu.VMEM((block_rows, 2 * HD), jnp.float32),
            ],
        ),
        out_shape=pltpu.HBM((sources, heads, out_clips, rows, HD), arrived.dtype),
        input_output_aliases={6: 0} if earlier else {},
        compiler_params=pltpu.CompilerParams(vmem_limit_bytes=VMEM_LIMIT),
        name="attend",
    )(in_hbm(lengths), group, place, arrived, arrived, arrived, *earlier)
    return attended


def unpack(lengths, group, parts, returned):
    heads, _, rows, _ = returned[0].shape
    per_group = sum(clips for _, clips in parts)

    def kernel(lengths_ref, group_ref, *refs):
        out_ref = refs[-1]
        rank = pl.program_id(0)
        for (first, clips), in_ref in zip(parts, refs):

            @pl.when((rank >= first) & (rank < first + clips))
            def _(in_ref=in_ref):
                def by_head(head, carry):
                    out_ref[0, :, pl.ds(pl.multiple_of(head * HD, HD), HD)] = in_ref[head, 0]
                    return carry

                lax.fori_loop(0, heads, by_head, 0, unroll=UNROLL)

    return pl.pallas_call(
        kernel,
        grid_spec=pltpu.PrefetchScalarGridSpec(
            num_scalar_prefetch=2,
            grid=(per_group,),
            in_specs=[
                pl.BlockSpec(
                    (heads, 1, rows, HD),
                    lambda c, ln, gr, first=first, clips=clips: (0, jnp.clip(c - first, 0, clips - 1), 0, 0),
                )
                for first, clips in parts
            ],
            out_specs=pl.BlockSpec(
                (1, rows, heads * HD), lambda c, ln, gr: (by_length(ln, gr, per_group, c)[0], 0, 0)
            ),
        ),
        out_shape=pltpu.HBM((per_group, rows, heads * HD), returned[0].dtype),
        compiler_params=pltpu.CompilerParams(vmem_limit_bytes=VMEM_LIMIT),
        name="unpack",
    )(in_hbm(lengths), group, *returned)


def exchange(array, peers):
    devices = lax.axis_size("seq")
    blocks = [list(range(start, start + peers)) for start in range(0, devices, peers)]
    return lax.all_to_all(
        array, "seq", split_axis=0, concat_axis=0, axis_index_groups=blocks, tiled=True
    )


def planned(*outputs, order):
    def run(queries, keys, values, lengths, group, place):
        per_group = queries.shape[0]
        arrived, before = {}, None
        for part in order:
            packed = pack(lengths, group, part[0], part[1], queries, keys, values)
            if before is not None:
                packed, arrived[before] = lax.optimization_barrier((packed, arrived[before]))
            arrived[part] = exchange(packed, part[2])
            before = part
        last = arrived[before]
        attended, places = [], []
        for output in outputs:
            first, total = output[0][0], sum(part[1] for part in output)
            places.append((first, total))
            results = None
            for part in output:
                if part != before:
                    results = attend(
                        lengths, group, place, *part, per_group, arrived[part], results, part[0] - first, total
                    )
            attended.append(results)
        attended, last = lax.optimization_barrier((attended, last))
        returned = []
        for output, (first, total), results in zip(outputs, places, attended):
            part, peers = output[-1], output[-1][2]
            if part == before:
                results = attend(
                    lengths, group, place, *part, per_group, arrived[part], results, part[0] - first, total
                )
            results = results.reshape(-1, *results.shape[2:])
            results, last = lax.optimization_barrier((results, last))
            last = exchange(results, peers)
            returned.append(last)
        return unpack(lengths, group, places, returned)

    return run


FOUR, PAIR, TINY_PAIR = (0, 4, NEAR), (0, 2, NEAR), (2, 2, NEAREST)
TWO, ONE, THREE, LAST = (0, 2, WIDE), (2, 1, WIDE), (0, 3, WIDE), (3, 1, WIDE)
LAST_PAIR, SHORT = (2, 2, NEAR), (3, 1, NEAR)
PLANS = [
    planned([FOUR], order=[FOUR]),
    planned([TINY_PAIR], [PAIR], order=[TINY_PAIR, PAIR]),
    planned([LAST_PAIR], [TWO], order=[LAST_PAIR, TWO]),
    planned([TWO], [LAST_PAIR], order=[TWO, LAST_PAIR]),
    planned([SHORT], [TWO, ONE], order=[SHORT, TWO, ONE]),
    planned([THREE], [SHORT], order=[THREE, SHORT]),
    planned([THREE, LAST], order=[THREE, LAST]),
    planned([LAST], [THREE], order=[LAST, THREE]),
]


def choose_plan(lengths, group, per_group, rows):
    def kernel(lengths_ref, group_ref, out_ref):
        mine = group_ref[0]
        odd = lax.rem(mine, 2)

        def how_many(which, test):
            return sum(
                test(lengths_ref[which * per_group + slot]).astype(jnp.int32) for slot in range(per_group)
            )

        long = how_many(mine, lambda length: length > NEAR * rows)
        tiny = how_many(mine, lambda length: length <= NEAREST * rows)
        beside = how_many(mine + 1 - 2 * odd, lambda length: length > NEAR * rows)
        differ = jnp.where(
            long == per_group, beside == per_group, (beside > 0) & (beside < per_group)
        )
        with_long = 2 * jnp.maximum(long - 1, 1) + odd * differ.astype(jnp.int32)
        out_ref[0] = jnp.where(long > 0, with_long, (tiny >= 2).astype(jnp.int32))

    return pl.pallas_call(
        kernel,
        grid_spec=pltpu.PrefetchScalarGridSpec(
            num_scalar_prefetch=2,
            grid=(),
            in_specs=[],
            out_specs=pl.BlockSpec(memory_space=pltpu.SMEM),
        ),
        out_shape=jax.ShapeDtypeStruct((1,), jnp.int32),
        name="choose_plan",
    )(in_hbm(lengths), group)


def local(queries, key_tokens, value_tokens, clip_lengths):
    per_group, rows = queries.shape[:2]
    group, place = lax.axis_index("grp").reshape(1), lax.axis_index("seq").reshape(1)
    return lax.switch(
        choose_plan(clip_lengths, group, per_group, rows)[0],
        PLANS,
        queries, key_tokens, value_tokens, clip_lengths, group, place,
    )


def solution(mesh):
    in_specs = (P("grp", "seq", None), P("grp", "seq", None), P("grp", "seq", None), P())
    out_specs = P("grp", "seq", None)
    return jax.shard_map(local, mesh=mesh, in_specs=in_specs, out_specs=out_specs, check_vma=False)
```

```python
import jax
import jax.numpy as jnp
from jax import lax
from jax.experimental import pallas as pl
from jax.experimental.pallas import tpu as pltpu
from jax.sharding import PartitionSpec as P

HD = 128
EXP2_SCALE = HD ** (-0.5) * 1.4426950408889634
BLOCK = 512
PIECE = 64
UNROLL = 4
WIDE, NEAR, NEAREST = 32, 8, 4
VMEM_LIMIT = 24 * 2**20


def in_hbm(array):
    return pltpu.with_memory_space_constraint(array, pltpu.HBM)


def by_length(lengths_ref, group_ref, per_group, rank):
    lengths = [lengths_ref[group_ref[0] * per_group + slot] for slot in range(per_group)]
    slot_at_rank, length_at_rank = jnp.int32(0), jnp.int32(0)
    for slot in range(per_group):
        place = jnp.int32(0)
        for other in range(per_group):
            if other < slot:
                place += (lengths[other] >= lengths[slot]).astype(jnp.int32)
            elif other > slot:
                place += (lengths[other] > lengths[slot]).astype(jnp.int32)
        slot_at_rank = jnp.where(place == rank, slot, slot_at_rank)
        length_at_rank = jnp.where(place == rank, lengths[slot], length_at_rank)
    return slot_at_rank, length_at_rank


def pack(lengths, group, first, clips, queries, keys, values):
    per_group, rows, features = queries.shape
    heads = features // HD

    def kernel(lengths_ref, group_ref, q_ref, k_ref, v_ref, out_ref, held, sems):
        def fetch(clip, slot, position):
            source = (q_ref, k_ref, v_ref)[position].at[slot]
            return pltpu.make_async_copy(source, held.at[clip, position], sems.at[clip, position])

        clip = pl.program_id(0)

        @pl.when(clip == 0)
        def _():
            for each in range(clips):
                slot = by_length(lengths_ref, group_ref, per_group, first + each)[0]
                for position in range(3):
                    fetch(each, slot, position).start()

        for position in range(3):
            fetch(clip, 0, position).wait()

        def by_head(head, carry):
            columns = pl.ds(pl.multiple_of(head * HD, HD), HD)
            for position in range(3):
                out_ref[head, position, 0] = held[clip, position, :, columns]
            return carry

        lax.fori_loop(0, heads, by_head, 0, unroll=UNROLL)

    return pl.pallas_call(
        kernel,
        grid_spec=pltpu.PrefetchScalarGridSpec(
            num_scalar_prefetch=2,
            grid=(clips,),
            in_specs=[pl.BlockSpec(memory_space=pltpu.HBM)] * 3,
            out_specs=pl.BlockSpec((heads, 3, 1, rows, HD), lambda c, ln, gr: (0, 0, c, 0, 0)),
            scratch_shapes=[
                pltpu.VMEM((clips, 3, rows, features), queries.dtype),
                pltpu.SemaphoreType.DMA((clips, 3)),
            ],
        ),
        out_shape=pltpu.HBM((heads, 3, clips, rows, HD), queries.dtype),
        compiler_params=pltpu.CompilerParams(vmem_limit_bytes=VMEM_LIMIT),
        name="pack",
    )(in_hbm(lengths), group, in_hbm(queries), in_hbm(keys), in_hbm(values))


def attend_head(head, count, q_ref, k_ref, v_ref, out_ref, scratch):
    values_ref, keys_ref, score_ref, max_ref, weight_ref, summed_ref = scratch
    rows_each = q_ref.shape[4]
    block_rows = score_ref.shape[1]
    pieces = block_rows // rows_each
    blocks = (count + block_rows - 1) // block_rows

    def score_block(query_rows, block, masked):
        scores = jnp.dot(query_rows, keys_ref[block], preferred_element_type=jnp.float32)
        if masked:
            columns = block * block_rows + lax.broadcasted_iota(jnp.int32, (1, block_rows), 1)
            scores = jnp.where(columns < count, scores, -jnp.inf)
        score_ref[block] = scores
        lane_max = scores[:, :HD]
        for start in range(HD, block_rows, HD):
            lane_max = jnp.maximum(lane_max, scores[:, start : start + HD])
        max_ref[...] = jnp.maximum(max_ref[...], lane_max)

    def weight_block(block, carry):
        value_rows = values_ref[pl.ds(pl.multiple_of(block * block_rows, block_rows), block_rows)]
        for row in range(0, block_rows, PIECE):
            rows = slice(row, row + PIECE)
            row_max = max_ref[rows, :]
            for start in range(0, block_rows, HD):
                scores = score_ref[block, rows, start : start + HD]
                weights = jnp.exp2((scores - row_max) * EXP2_SCALE)
                weight_ref[rows, start : start + HD] = weights.astype(weight_ref.dtype)
        summed_ref[...] += jnp.dot(weight_ref[...], value_rows, preferred_element_type=jnp.float32)
        return carry

    def tile(step, carry):
        at = pl.ds(step * pieces, pieces)
        query_rows = q_ref[at, head].reshape(block_rows, HD)
        max_ref[...] = jnp.full_like(max_ref, -jnp.inf)

        def whole_block(block, inner):
            score_block(query_rows, block, False)
            return inner

        lax.fori_loop(0, blocks - 1, whole_block, 0)
        score_block(query_rows, blocks - 1, True)
        max_ref[...] = jnp.broadcast_to(jnp.max(max_ref[...], axis=1, keepdims=True), max_ref.shape)
        summed_ref[...] = jnp.zeros_like(summed_ref)
        lax.fori_loop(0, blocks, weight_block, 0)
        rows = step * block_rows + lax.broadcasted_iota(jnp.int32, (block_rows, HD), 0)
        attended = jnp.where(rows < count, summed_ref[:, :HD] / summed_ref[:, HD:], 0.0)
        out_ref[at, head] = attended.astype(out_ref.dtype).reshape(pieces, 1, rows_each, HD)
        return carry

    def turn_block(block, carry):
        key_rows = k_ref[pl.ds(block * pieces, pieces), head].reshape(block_rows, HD)
        keys_ref[block] = key_rows.T
        return carry

    lax.fori_loop(0, blocks, turn_block, 0)
    values_ref[:, :HD] = v_ref[:, head].reshape(values_ref.shape[0], HD)
    lax.fori_loop(0, blocks, tile, 0)


def attend(lengths, group, place, first, clips, sources, per_group, arrived, into, out_first, out_clips):
    earlier = [] if into is None else [in_hbm(into)]
    heads, rows = arrived.shape[0] // sources, arrived.shape[3]
    held_rows = sources * rows
    block_rows = min(BLOCK, held_rows)
    arrived = arrived.reshape(sources, heads, 3, clips, rows, HD)
    whole = lambda position: pl.BlockSpec(
        (sources, heads, 1, 1, rows, HD), lambda c, ln, gr, at: (0, 0, position, c, 0, 0)
    )

    def kernel(lengths_ref, group_ref, place_ref, q_ref, k_ref, v_ref, *refs):
        out_ref, *scratch = refs[len(earlier) :]
        count = by_length(lengths_ref, group_ref, per_group, first + pl.program_id(0))[1]
        count = jnp.where(place_ref[0] < sources, count, 0)
        out_ref[...] = jnp.zeros_like(out_ref)

        @pl.when(pl.program_id(0) == 0)
        def _():
            scratch[0][:, HD:] = jnp.ones((held_rows, HD), scratch[0].dtype)

        def by_head(head, carry):
            attend_head(head, count, q_ref, k_ref, v_ref, out_ref, scratch)
            return carry

        @pl.when(count > 0)
        def _():
            lax.fori_loop(0, heads, by_head, 0)

    attended = pl.pallas_call(
        kernel,
        grid_spec=pltpu.PrefetchScalarGridSpec(
            num_scalar_prefetch=3,
            grid=(clips,),
            in_specs=[whole(0), whole(1), whole(2)] + [pl.BlockSpec(memory_space=pl.ANY)] * len(earlier),
            out_specs=pl.BlockSpec(
                (sources, heads, 1, rows, HD), lambda c, ln, gr, at: (0, 0, c + out_first, 0, 0)
            ),
            scratch_shapes=[
                pltpu.VMEM((held_rows, 2 * HD), arrived.dtype),
                pltpu.VMEM((held_rows // block_rows, HD, block_rows), arrived.dtype),
                pltpu.VMEM((held_rows // block_rows, block_rows, block_rows), jnp.float32),
                pltpu.VMEM((block_rows, HD), jnp.float32),
                pltpu.VMEM((block_rows, block_rows), arrived.dtype),
                pltpu.VMEM((block_rows, 2 * HD), jnp.float32),
            ],
        ),
        out_shape=pltpu.HBM((sources, heads, out_clips, rows, HD), arrived.dtype),
        input_output_aliases={6: 0} if earlier else {},
        compiler_params=pltpu.CompilerParams(vmem_limit_bytes=VMEM_LIMIT),
        name="attend",
    )(in_hbm(lengths), group, place, arrived, arrived, arrived, *earlier)
    return attended


def unpack(lengths, group, parts, returned):
    heads, _, rows, _ = returned[0].shape
    per_group = sum(clips for _, clips in parts)

    def kernel(lengths_ref, group_ref, *refs):
        out_ref = refs[-1]
        rank = pl.program_id(0)
        for (first, clips), in_ref in zip(parts, refs):

            @pl.when((rank >= first) & (rank < first + clips))
            def _(in_ref=in_ref):
                def by_head(head, carry):
                    out_ref[0, :, pl.ds(pl.multiple_of(head * HD, HD), HD)] = in_ref[head, 0]
                    return carry

                lax.fori_loop(0, heads, by_head, 0, unroll=UNROLL)

    return pl.pallas_call(
        kernel,
        grid_spec=pltpu.PrefetchScalarGridSpec(
            num_scalar_prefetch=2,
            grid=(per_group,),
            in_specs=[
                pl.BlockSpec(
                    (heads, 1, rows, HD),
                    lambda c, ln, gr, first=first, clips=clips: (0, jnp.clip(c - first, 0, clips - 1), 0, 0),
                )
                for first, clips in parts
            ],
            out_specs=pl.BlockSpec(
                (1, rows, heads * HD), lambda c, ln, gr: (by_length(ln, gr, per_group, c)[0], 0, 0)
            ),
        ),
        out_shape=pltpu.HBM((per_group, rows, heads * HD), returned[0].dtype),
        compiler_params=pltpu.CompilerParams(vmem_limit_bytes=VMEM_LIMIT),
        name="unpack",
    )(in_hbm(lengths), group, *returned)


def exchange(array, peers):
    devices = lax.axis_size("seq")
    blocks = [list(range(start, start + peers)) for start in range(0, devices, peers)]
    return lax.all_to_all(
        array, "seq", split_axis=0, concat_axis=0, axis_index_groups=blocks, tiled=True
    )


def planned(*outputs, order):
    def run(queries, keys, values, lengths, group, place):
        per_group = queries.shape[0]
        arrived, before = {}, None
        for part in order:
            packed = pack(lengths, group, part[0], part[1], queries, keys, values)
            if before is not None:
                packed, arrived[before] = lax.optimization_barrier((packed, arrived[before]))
            if before is None and part[2] != WIDE:
                arrived[part] = lax.cond(
                    place[0] < part[2], lambda rows, peers=part[2]: exchange(rows, peers), lambda rows: rows, packed
                )
            else:
                arrived[part] = exchange(packed, part[2])
            before = part
        last = arrived[before]
        attended, places = [], []
        for output in outputs:
            first, total = output[0][0], sum(part[1] for part in output)
            places.append((first, total))
            results = None
            for part in output:
                if part != before:
                    results = attend(
                        lengths, group, place, *part, per_group, arrived[part], results, part[0] - first, total
                    )
            attended.append(results)
        attended, last = lax.optimization_barrier((attended, last))
        returned = []
        for output, (first, total), results in zip(outputs, places, attended):
            part, peers = output[-1], output[-1][2]
            if part == before:
                results = attend(
                    lengths, group, place, *part, per_group, arrived[part], results, part[0] - first, total
                )
            results = results.reshape(-1, *results.shape[2:])
            results, last = lax.optimization_barrier((results, last))
            last = exchange(results, peers)
            returned.append(last)
        return unpack(lengths, group, places, returned)

    return run


FOUR, PAIR, TINY_PAIR = (0, 4, NEAR), (0, 2, NEAR), (2, 2, NEAREST)
TWO, ONE, THREE, LAST = (0, 2, WIDE), (2, 1, WIDE), (0, 3, WIDE), (3, 1, WIDE)
LAST_PAIR, SHORT = (2, 2, NEAR), (3, 1, NEAR)
PLANS = [
    planned([FOUR], order=[FOUR]),
    planned([TINY_PAIR], [PAIR], order=[TINY_PAIR, PAIR]),
    planned([LAST_PAIR], [TWO], order=[LAST_PAIR, TWO]),
    planned([TWO], [LAST_PAIR], order=[TWO, LAST_PAIR]),
    planned([SHORT], [TWO, ONE], order=[SHORT, TWO, ONE]),
    planned([THREE], [SHORT], order=[THREE, SHORT]),
    planned([THREE, LAST], order=[THREE, LAST]),
    planned([LAST], [THREE], order=[LAST, THREE]),
]


def choose_plan(lengths, group, per_group, rows):
    def kernel(lengths_ref, group_ref, out_ref):
        mine = group_ref[0]
        odd = lax.rem(mine, 2)

        def how_many(which, test):
            return sum(
                test(lengths_ref[which * per_group + slot]).astype(jnp.int32) for slot in range(per_group)
            )

        long = how_many(mine, lambda length: length > NEAR * rows)
        tiny = how_many(mine, lambda length: length <= NEAREST * rows)
        beside = how_many(mine + 1 - 2 * odd, lambda length: length > NEAR * rows)
        differ = jnp.where(
            long == per_group, beside == per_group, (beside > 0) & (beside < per_group)
        )
        with_long = 2 * jnp.maximum(long - 1, 1) + odd * differ.astype(jnp.int32)
        out_ref[0] = jnp.where(long > 0, with_long, (tiny >= 2).astype(jnp.int32))

    return pl.pallas_call(
        kernel,
        grid_spec=pltpu.PrefetchScalarGridSpec(
            num_scalar_prefetch=2,
            grid=(),
            in_specs=[],
            out_specs=pl.BlockSpec(memory_space=pltpu.SMEM),
        ),
        out_shape=jax.ShapeDtypeStruct((1,), jnp.int32),
        name="choose_plan",
    )(in_hbm(lengths), group)


def local(queries, key_tokens, value_tokens, clip_lengths):
    per_group, rows = queries.shape[:2]
    group, place = lax.axis_index("grp").reshape(1), lax.axis_index("seq").reshape(1)
    return lax.switch(
        choose_plan(clip_lengths, group, per_group, rows)[0],
        PLANS,
        queries, key_tokens, value_tokens, clip_lengths, group, place,
    )


def solution(mesh):
    in_specs = (P("grp", "seq", None), P("grp", "seq", None), P("grp", "seq", None), P())
    out_specs = P("grp", "seq", None)
    return jax.shard_map(local, mesh=mesh, in_specs=in_specs, out_specs=out_specs, check_vma=False)
```
